32 devices in a mesh: wide: 8 (over z, core), blk: 4 (over y, x).
Axes of the slice: x: 2, y: 2, z: 4, core: 2. Of those that a mesh axis runs over, the one named last changes fastest.
Arguments:
- queries: bfloat16 [128, 64, 512], P(('wide', 'blk')), may hold values from -6 to 6
- references: bfloat16 [64, 64, 512], P(('wide', 'blk')), may hold values from -6 to 6
- query_taps: bfloat16 [16, 9], replicated, may hold values from -2 to 2
- ref_taps: bfloat16 [16, 9], replicated, may hold values from -0.5 to 0.5
- tap_bias: float32 [16], replicated, may hold values from -3 to 3
- candidates: int32 [32, 8], P(('wide', 'blk')), may hold values 0 or 1
Outputs:
- scores: float32 [128, 64], P(('wide', 'blk'))
The draws below stay inside these ranges and needn't reach their ends.
All inputs are finite; a program needn't handle non-finite values. No bound on the sum of `candidates` on one device may be relied on, other than what follows from the above.
Results may differ from the reference program's by a relative error of at most 0.0006.
Values may be sent and summed in bfloat16 or wider, within the bound.
A program may use at most 64 MiB of HBM per device.

```python
import math
import jax
import jax.numpy as jnp
from jax import lax

SIDE = 8
C = 512
HID = 16
QT = 4
CELLS = 64
TILES = 32
BLOCKS = 8
BR = 8
NQ = 128
NR = 64


def plant(values, own_key, low, high):
    place = [jax.random.randint(jax.random.fold_in(own_key, axis), (), 0, length) for axis, length in enumerate(values.shape)]
    main_axis = values.shape.index(max(values.shape))
    neighbour = place[:main_axis] + [(place[main_axis] + 1) % values.shape[main_axis]] + place[main_axis + 1:]
    return values.at[tuple(place)].set(low).at[tuple(neighbour)].set(high)


def levels(key, shape, split, least, high):
    loudness = 1.0
    for axis_at, shards_of in split:
        steps = jax.random.uniform(jax.random.fold_in(jax.random.fold_in(key, 6), axis_at), (shards_of,), jnp.float32, least / len(split), high / len(split))
        loudness = loudness * jnp.repeat(jnp.exp(steps), shape[axis_at] // shards_of).reshape((-1,) + (1,) * (len(shape) - 1 - axis_at))
    return loudness


def bell_draw(own_key, dims, deviation, limit, split=(), held_as=jnp.bfloat16):
    values = deviation * jax.random.normal(own_key, dims, jnp.float32)
    if split:
        values = values * levels(own_key, dims, split, -0.22, 0.18)
    return jnp.clip(values, -limit, limit).astype(held_as)


def setup_inputs(seed: int = 0) -> dict:
    key_of = jax.random.split(jax.random.key(seed), 7)
    queries = bell_draw(key_of[0], (NQ, CELLS, C), 1.0, 6.0, ((0, 32),))
    references = bell_draw(key_of[1], (NR, CELLS, C), 1.0, 6.0, ((0, 32),))
    query_taps = bell_draw(key_of[2], (HID, 9), 9 ** -0.5, 2.0)
    ref_taps = bell_draw(key_of[3], (HID, 9), (9 * HID) ** -0.5, 0.5)
    tap_bias = bell_draw(key_of[4], (HID,), 0.5, 3.0, (), jnp.float32)
    candidates = plant((jax.random.randint(key_of[5], (TILES, BLOCKS), 0, 2) < 1).astype(jnp.int32), jax.random.fold_in(key_of[5], 1), 0, 1)
    return {"queries": queries, "references": references, "query_taps": query_taps, "ref_taps": ref_taps, "tap_bias": tap_bias, "candidates": candidates}


epsilon = 1e-06

def conv_table(weights, width):
    count = width * width
    position = jnp.arange(count, dtype=jnp.int32)
    grid_row = position // width
    grid_col = position % width
    delta_row = grid_row[None, :] - grid_row[:, None]
    delta_col = grid_col[None, :] - grid_col[:, None]
    inside = (jnp.abs(delta_row) <= 1) & (jnp.abs(delta_col) <= 1)
    tap_index = (delta_row + 1) * 3 + (delta_col + 1)
    selector = (tap_index[None] == jnp.arange(9, dtype=jnp.int32)[:, None, None]) & inside[None]
    table = lax.optimization_barrier(jnp.sum(jnp.where(selector[None], weights.astype(jnp.float32)[:, :, None, None], jnp.float32(0.0)), axis=1))
    return table.astype(jnp.bfloat16)

def normalize(features):
    values = features.astype(jnp.float32)
    inverse_rms = lax.rsqrt(lax.optimization_barrier(jnp.mean(values * values, axis=-1, keepdims=True)) + epsilon)
    return (values * inverse_rms).astype(jnp.bfloat16)

def pair_scores(query_unit, ref_unit, query_table, ref_table, tap_bias):
    count = query_unit.shape[0]
    others = ref_unit.shape[0]
    cell_count = query_unit.shape[1]
    depth = query_unit.shape[2]
    correlation = jnp.dot(query_unit.reshape(count * cell_count, depth), ref_unit.reshape(others * cell_count, depth).T, preferred_element_type=jnp.float32)
    correlation = (correlation / math.sqrt(depth)).astype(jnp.bfloat16).reshape(count, cell_count, others, cell_count)
    hidden = jnp.einsum('kai,pirj->pkarj', query_table.astype(jnp.float32), correlation.astype(jnp.float32))
    hidden = jnp.maximum(hidden + tap_bias[None, :, None, None, None], 0.0).astype(jnp.bfloat16)
    filtered = jnp.einsum('pkarj,kbj->parb', hidden.astype(jnp.float32), ref_table.astype(jnp.float32))
    row_pool = lax.optimization_barrier(jnp.mean(lax.optimization_barrier(jnp.max(filtered, axis=3)), axis=1))
    col_pool = lax.optimization_barrier(jnp.mean(lax.optimization_barrier(jnp.max(filtered, axis=1)), axis=2))
    return 0.5 * (row_pool + col_pool)

def reference(queries, references, query_taps, ref_taps, tap_bias, candidates):
    query_table = conv_table(query_taps, SIDE)
    ref_table = conv_table(ref_taps, SIDE)
    query_unit = normalize(queries).reshape(TILES, QT, CELLS, C)
    ref_unit = normalize(references).reshape(BLOCKS, BR, CELLS, C)

    def per_tile(query_tile):

        def per_block(ref_block):
            return pair_scores(query_tile, ref_block, query_table, ref_table, tap_bias)
        return lax.map(per_block, ref_unit)
    scores = lax.map(per_tile, query_unit)
    scores = jnp.transpose(scores, (0, 2, 1, 3))
    keep = candidates[:, None, :, None] != 0
    return jnp.where(keep, scores, jnp.float32(0.0)).reshape(NQ, NR).astype(jnp.float32)
```

```python
import functools
import math

import jax
import jax.numpy as jnp
from jax import lax
from jax.experimental import pallas as pl
from jax.experimental.pallas import tpu as pltpu
from jax.sharding import PartitionSpec as P

SIDE = 8
EPS = 1e-06
GROUP = 4
MESH = pl.DeviceIdType.MESH
VMEM = pl.BlockSpec(memory_space=pltpu.VMEM)
SMEM = pl.BlockSpec(memory_space=pltpu.SMEM)


def normalize(values):
    values = values.astype(jnp.float32)
    inverse_rms = lax.rsqrt(jnp.mean(values * values, axis=-1, keepdims=True) + EPS)
    return (values * inverse_rms).astype(jnp.bfloat16)


def tap_masks(rows, lanes, outer_on_rows):
    row = lax.broadcasted_iota(jnp.int32, (rows, lanes), 0) % (SIDE * SIDE)
    lane = lax.broadcasted_iota(jnp.int32, (rows, lanes), 1) % (SIDE * SIDE)
    out_cell, in_cell = (row, lane) if outer_on_rows else (lane, row)
    dy = in_cell // SIDE - out_cell // SIDE
    dx = in_cell % SIDE - out_cell % SIDE
    return [(dy == t // 3 - 1) & (dx == t % 3 - 1) for t in range(9)]


def gather_kernel(nw, nb, q_ref, r_ref, qt_ref, rt_ref, cand_ref,
                  corr_ref, qtab_ref, rtab_ref, call_ref,
                  qall, rall, qs, qr, rs, rr, cs, cr):
    w, b = lax.axis_index("wide"), lax.axis_index("blk")
    cells = q_ref.shape[1]
    depth = q_ref.shape[2]
    nq, nr = q_ref.shape[0], r_ref.shape[0]
    hid = qt_ref.shape[0]

    barrier = pltpu.get_barrier_semaphore()
    for d in range(1, nb):
        pl.semaphore_signal(barrier, inc=1, device_id=(w, lax.rem(b + d, nb)), device_id_type=MESH)
    for d in range(1, nw):
        pl.semaphore_signal(barrier, inc=1, device_id=(lax.rem(w + d, nw), b), device_id_type=MESH)
    qall[b] = normalize(q_ref[...]).reshape(nq * cells, depth)
    rall[w] = normalize(r_ref[...]).reshape(nr * cells, depth)
    call_ref[b] = cand_ref[...]
    pl.semaphore_wait(barrier, nb + nw - 2)

    copies = []
    for d in range(1, nb):
        copies.append(pltpu.make_async_remote_copy(
            src_ref=call_ref.at[b], dst_ref=call_ref.at[b], send_sem=cs.at[d], recv_sem=cr.at[d],
            device_id=(w, lax.rem(b + d, nb)), device_id_type=MESH))
    for d in range(1, max(nb, nw)):
        if d < nw:
            copies.append(pltpu.make_async_remote_copy(
                src_ref=rall.at[w], dst_ref=rall.at[w], send_sem=rs.at[d], recv_sem=rr.at[d],
                device_id=(lax.rem(w + d, nw), b), device_id_type=MESH))
        if d < nb:
            copies.append(pltpu.make_async_remote_copy(
                src_ref=qall.at[b], dst_ref=qall.at[b], send_sem=qs.at[d], recv_sem=qr.at[d],
                device_id=(w, lax.rem(b + d, nb)), device_id_type=MESH))
    for c in copies:
        c.start()

    taps = qt_ref[...].astype(jnp.float32)
    masks = tap_masks(cells, cells, True)
    for k in range(hid):
        table = jnp.zeros((cells, cells), jnp.float32)
        for t in range(9):
            table = jnp.where(masks[t], taps[k:k + 1, t:t + 1], table)
        qtab_ref[k * cells:(k + 1) * cells, :] = table.astype(jnp.bfloat16)
    taps = rt_ref[...].astype(jnp.float32)
    masks = tap_masks(cells, 2 * cells, False)
    left = lax.broadcasted_iota(jnp.int32, (cells, 2 * cells), 1) < cells
    rtab_ref[...] = jnp.zeros_like(rtab_ref)
    for k in range(hid):
        table = jnp.zeros((cells, 2 * cells), jnp.float32)
        for t in range(9):
            table = jnp.where(masks[t], taps[k:k + 1, t:t + 1], table)
        for s in range(4):
            row = (k * 4 + s) * cells
            half = s // 2 * 2 * cells
            part = jnp.where(left if s % 2 == 0 else ~left, table, 0.0)
            rtab_ref[row:row + cells, half:half + 2 * cells] = part.astype(jnp.bfloat16)

    for c in copies:
        c.wait()

    scale = 1.0 / math.sqrt(depth)

    def one(n, carry):
        t, v = n // nw, n % nw
        block = lax.dot_general(qall[t], rall[v], (((1,), (1,)), ((), ())),
                                preferred_element_type=jnp.float32)
        block = (block * scale).astype(jnp.bfloat16)
        for p in range(nq):
            corr_ref[n, :, p * nr * cells:(p + 1) * nr * cells] = block[p * cells:(p + 1) * cells]
        return carry

    lax.fori_loop(0, nb * nw, one, 0)


def score_kernel(nw, nb, nq, nr, cand_ref, bias_ref, corr_ref, qtab_ref, rtab_ref, out_ref, hidden, items):
    b = lax.axis_index("blk")
    cells = corr_ref.shape[1]
    hid = bias_ref.shape[0]
    wide = 4 * cells
    out_ref[...] = jnp.zeros_like(out_ref)

    def scan(n, count):
        @pl.when(cand_ref[n // nw, 0, n % nw] != 0)
        def _():
            items[count] = n
        return count + jnp.where(cand_ref[n // nw, 0, n % nw] != 0, 1, 0)

    count = lax.fori_loop(0, nb * nw, scan, jnp.int32(0))
    columns = out_ref.shape[2]
    halves = nq * nr // 4
    row_id = lax.broadcasted_iota(jnp.int32, (nq, columns), 0)
    lane_id = lax.broadcasted_iota(jnp.int32, (nq, columns), 1)
    left = lax.broadcasted_iota(jnp.int32, (cells, 2 * cells), 1) < cells
    left_row = lax.broadcasted_iota(jnp.int32, (1, 2 * cells), 1) < cells

    def group(i, carry):
        own = [items[jnp.minimum(i * GROUP + g, count - 1)] for g in range(GROUP)]
        for g in range(GROUP):
            for h in range(halves):
                value = jnp.dot(qtab_ref[...], corr_ref[own[g], :, h * wide:(h + 1) * wide],
                                preferred_element_type=jnp.float32)
                row = (g * halves + h) * cells
                for k in range(hid):
                    part = value[k * cells:(k + 1) * cells] + bias_ref[k]
                    hidden[row:row + cells, k * wide:(k + 1) * wide] = jnp.maximum(part, 0.0).astype(jnp.bfloat16)
        filtered = jnp.dot(hidden[...], rtab_ref[...], preferred_element_type=jnp.float32)
        for g in range(GROUP):
            t, v = own[g] // nw, own[g] % nw
            base = v * (nb * nr) + b * nr
            result = out_ref[t]
            for p in range(nq):
                row = (g * halves + p // 2) * cells
                lane = p % 2 * 2 * cells
                f = filtered[row:row + cells, lane:lane + 2 * cells]
                col = jnp.max(f, axis=0, keepdims=True)
                for r in range(2):
                    own_f = jnp.where(left if r == 0 else ~left, f, -jnp.inf)
                    own_c = jnp.where(left_row if r == 0 else ~left_row, col, 0.0)
                    total = (jnp.sum(jnp.max(own_f, axis=1, keepdims=True), axis=0, keepdims=True)
                             + jnp.sum(own_c, axis=1, keepdims=True))
                    total = total * (0.5 / cells)
                    result = jnp.where((row_id == p) & (lane_id == base + r), total, result)
            out_ref[t] = result
        return carry

    lax.fori_loop(0, (count + GROUP - 1) // GROUP, group, 0)


def exchange_kernel(nw, nb, s_ref, out_ref, got, ss, sr):
    w, b = lax.axis_index("wide"), lax.axis_index("blk")
    barrier = pltpu.get_barrier_semaphore()
    for d in range(1, nb):
        pl.semaphore_signal(barrier, inc=1, device_id=(w, lax.rem(b + d, nb)), device_id_type=MESH)
    pl.semaphore_wait(barrier, nb - 1)
    copies = []
    for d in range(1, nb):
        to = lax.rem(b + d, nb)
        copies.append(pltpu.make_async_remote_copy(
            src_ref=s_ref.at[to], dst_ref=got.at[d], send_sem=ss.at[d], recv_sem=sr.at[d],
            device_id=(w, to), device_id_type=MESH))
    for c in copies:
        c.start()
    total = s_ref[b]
    for c in copies:
        c.wait()
    for d in range(1, nb):
        total = total + got[d]
    out_ref[...] = total


def shards(nw, nb, queries, references, query_taps, ref_taps, tap_bias, candidates):
    nq, cells, depth = queries.shape
    nr = references.shape[0]
    hid = query_taps.shape[0]
    dma = pltpu.SemaphoreType.DMA
    corr, qtab, rtab, cand = pl.pallas_call(
        functools.partial(gather_kernel, nw, nb),
        out_shape=(
            jax.ShapeDtypeStruct((nb * nw, cells, nq * nr * cells), jnp.bfloat16),
            jax.ShapeDtypeStruct((hid * cells, cells), jnp.bfloat16),
            jax.ShapeDtypeStruct((hid * 4 * cells, 4 * cells), jnp.bfloat16),
            jax.ShapeDtypeStruct((nb, 1, nw), jnp.int32),
        ),
        in_specs=[VMEM] * 5,
        out_specs=(VMEM,) * 4,
        scratch_shapes=[
            pltpu.VMEM((nb, nq * cells, depth), jnp.bfloat16),
            pltpu.VMEM((nw, nr * cells, depth), jnp.bfloat16),
            dma((nb,)), dma((nb,)), dma((nw,)), dma((nw,)), dma((nb,)), dma((nb,)),
        ],
        compiler_params=pltpu.CompilerParams(
            collective_id=0, has_side_effects=True, vmem_limit_bytes=48 * 2**20),
        name="gather",
    )(queries, references, query_taps, ref_taps, candidates)
    scores = pl.pallas_call(
        functools.partial(score_kernel, nw, nb, nq, nr),
        out_shape=jax.ShapeDtypeStruct((nb, nq, nw * nb * nr), jnp.float32),
        in_specs=[SMEM, SMEM, VMEM, VMEM, VMEM],
        out_specs=VMEM,
        scratch_shapes=[
            pltpu.VMEM((GROUP * nq * nr // 4 * cells, hid * 4 * cells), jnp.bfloat16),
            pltpu.SMEM((nb * nw,), jnp.int32),
        ],
        compiler_params=pltpu.CompilerParams(vmem_limit_bytes=48 * 2**20),
        name="score",
    )(cand, tap_bias, corr, qtab, rtab)
    return pl.pallas_call(
        functools.partial(exchange_kernel, nw, nb),
        out_shape=jax.ShapeDtypeStruct(scores.shape[1:], jnp.float32),
        in_specs=[VMEM],
        out_specs=VMEM,
        scratch_shapes=[pltpu.VMEM(scores.shape, jnp.float32), dma((nb,)), dma((nb,))],
        compiler_params=pltpu.CompilerParams(collective_id=1, has_side_effects=True),
        name="exchange",
    )(scores)


def solution(mesh):
    nw, nb = mesh.shape["wide"], mesh.shape["blk"]
    placed = (
        P(("wide", "blk"), None, None),
        P(("wide", "blk"), None, None),
        P(),
        P(),
        P(),
        P(("wide", "blk"), None),
    )
    return jax.shard_map(
        functools.partial(shards, nw, nb), mesh=mesh, in_specs=placed,
        out_specs=P(("wide", "blk"), None), check_vma=False,
    )
```

```python
import functools
import math

import jax
import jax.numpy as jnp
from jax import lax
from jax.experimental import pallas as pl
from jax.experimental.pallas import tpu as pltpu
from jax.sharding import PartitionSpec as P

SIDE = 8
EPS = 1e-06
GROUP = 4
MESH = pl.DeviceIdType.MESH
VMEM = pl.BlockSpec(memory_space=pltpu.VMEM)
HBM = pl.BlockSpec(memory_space=pltpu.HBM)
SMEM = pl.BlockSpec(memory_space=pltpu.SMEM)


def normalize(values):
    values = values.astype(jnp.float32)
    inverse_rms = lax.rsqrt(jnp.mean(values * values, axis=-1, keepdims=True) + EPS)
    return (values * inverse_rms).astype(jnp.bfloat16)


def tap_masks(rows, lanes, outer_on_rows):
    row = lax.broadcasted_iota(jnp.int32, (rows, lanes), 0) % (SIDE * SIDE)
    lane = lax.broadcasted_iota(jnp.int32, (rows, lanes), 1) % (SIDE * SIDE)
    out_cell, in_cell = (row, lane) if outer_on_rows else (lane, row)
    dy = in_cell // SIDE - out_cell // SIDE
    dx = in_cell % SIDE - out_cell % SIDE
    return [(dy == t // 3 - 1) & (dx == t % 3 - 1) for t in range(9)]


def gather_kernel(nw, nb, q_hbm, r_hbm, qt_hbm, rt_hbm, bias_hbm, cand_hbm,
                  corr_ref, qtab_ref, rtab_ref, call_ref,
                  qall, rall, qin, rin, qt_in, rt_in, bias_in,
                  load, qs, qr, zs, zr, ss, sr, cs, cr):
    w, b = lax.axis_index("wide"), lax.axis_index("blk")
    nz = nw // 2
    z, core = w // 2, w % 2
    twin = w + 1 - 2 * core
    nq, cells, depth = q_hbm.shape
    nr = r_hbm.shape[0]
    hid = qt_hbm.shape[0]
    last = nz - 1

    loads = [pltpu.make_async_copy(src, dst, load.at[n]) for n, (src, dst) in enumerate((
        (r_hbm, rin), (q_hbm, qin), (cand_hbm, call_ref.at[b]),
        (qt_hbm, qt_in), (rt_hbm, rt_in), (bias_hbm, bias_in)))]
    for c in loads:
        c.start()

    def signal(where):
        pl.semaphore_signal(barrier, inc=1, device_id=where, device_id_type=MESH)

    barrier = pltpu.get_barrier_semaphore()
    for d in range(1, nb):
        signal((w, lax.rem(b + d, nb)))
    signal((twin, b))

    @pl.when(z > 0)
    def _():
        signal((w - 2, b))

    @pl.when(z < last)
    def _():
        signal((w + 2, b))

    loads[0].wait()
    rall[w] = normalize(rin[...]).reshape(nr * cells, depth)
    loads[1].wait()
    qall[b] = normalize(qin[...]).reshape(nq * cells, depth)
    for c in loads[2:]:
        c.wait()
    pl.semaphore_wait(barrier, nb + jnp.where(z > 0, 1, 0) + jnp.where(z < last, 1, 0))

    def remote(ref, send, recv, n, where):
        return pltpu.make_async_remote_copy(
            src_ref=ref, dst_ref=ref, send_sem=send.at[n], recv_sem=recv.at[n],
            device_id=where, device_id_type=MESH)

    def up(s):
        return remote(rall.at[w - 2 * s], zs, zr, s, (jnp.minimum(w + 2, nw - 2 + core), b))

    def up_in(s):
        return remote(rall.at[w - 2 * s - 2], zs, zr, s, (twin, b))

    def down(s):
        return remote(rall.at[w + 2 * s], zs, zr, nz + s, (jnp.maximum(w - 2, core), b))

    def down_in(s):
        return remote(rall.at[w + 2 * s + 2], zs, zr, nz + s, (twin, b))

    def hand(owner, n):
        return remote(rall.at[owner], ss, sr, n, (twin, b))

    def line_step(s):
        @pl.when(z - 1 - s >= 0)
        def _():
            up_in(s).wait_recv()
            if s + 1 < last:
                @pl.when(z < last)
                def _():
                    up(s + 1).start()
            hand(w - 2 * s - 2, 1 + s).start()

        @pl.when(z + 1 + s <= last)
        def _():
            down_in(s).wait_recv()
            if s + 1 < last:
                @pl.when(z > 0)
                def _():
                    down(s + 1).start()
            hand(w + 2 * s + 2, nz + s).start()

    def hand_step(s):
        @pl.when(z - 1 - s >= 0)
        def _():
            hand(twin - 2 * s - 2, 1 + s).wait_recv()

        @pl.when(z + 1 + s <= last)
        def _():
            hand(twin + 2 * s + 2, nz + s).wait_recv()

    square = nb == 4
    half = nq * cells // 2
    bx, by = b % 2, b // 2 % 2
    on_x, on_y, across = b + 1 - 2 * bx, b + 2 - 4 * by, nb - 1 - b

    def piece(owner, h, n, where):
        return remote(qall.at[owner, h * half:(h + 1) * half], qs, qr, n, (w, where))

    small = [remote(call_ref.at[b], cs, cr, d, (w, lax.rem(b + d, nb))) for d in range(1, nb)]
    if square:
        first = [piece(b, 0, 0, on_x), piece(b, 1, 2, on_y), piece(b, 1, 1, on_x), piece(b, 0, 3, on_y)]
        onward = [piece(on_x, 0, 4, on_y), piece(on_y, 1, 5, on_x)]
        arrive = [piece(on_x, 0, 0, on_x), piece(on_y, 1, 2, on_y), piece(on_x, 1, 1, on_x),
                  piece(on_y, 0, 3, on_y), piece(across, 0, 4, on_y), piece(across, 1, 5, on_x)]
    else:
        first = [remote(qall.at[b], qs, qr, d, (w, lax.rem(b + d, nb))) for d in range(1, nb)]
        onward = []
        arrive = [remote(qall.at[lax.rem(b + nb - d, nb)], qs, qr, d, (w, lax.rem(b + d, nb)))
                  for d in range(1, nb)]

    @pl.when(z < last)
    def _():
        up(0).start()

    @pl.when(z > 0)
    def _():
        down(0).start()

    for c in first:
        c.start()
    hand(w, 0).start()
    for c in small:
        c.start()

    lane = lax.broadcasted_iota(jnp.int32, (cells, 2 * cells), 1)
    left = lane < cells
    columns = qtab_ref.shape[1]
    taps = qt_in[...].astype(jnp.float32)
    bias = bias_in[...]
    masks = [m & left for m in tap_masks(cells, 2 * cells, True)]
    for k in range(hid):
        b0 = jnp.broadcast_to(bias[:, k:k + 1], (cells, 2 * cells))
        b1 = b0.astype(jnp.bfloat16).astype(jnp.float32)
        b2 = (b0 - b1).astype(jnp.bfloat16).astype(jnp.float32)
        b3 = b0 - b1 - b2
        table = jnp.where(lane == cells, b1, jnp.where(lane == cells + 1, b2, jnp.where(lane == cells + 2, b3, 0.0)))
        for t in range(9):
            table = jnp.where(masks[t], taps[k:k + 1, t:t + 1], table)
        qtab_ref[k * cells:(k + 1) * cells, :] = table.astype(jnp.bfloat16)[:, :columns]
    taps = rt_in[...].astype(jnp.float32)
    masks = tap_masks(cells, 2 * cells, False)
    rtab_ref[...] = jnp.zeros_like(rtab_ref)
    for k in range(hid):
        table = jnp.zeros((cells, 2 * cells), jnp.float32)
        for t in range(9):
            table = jnp.where(masks[t], taps[k:k + 1, t:t + 1], table)
        for s in range(4):
            row = (k * 4 + s) * cells
            at = s // 2 * 2 * cells
            part = jnp.where(left if s % 2 == 0 else ~left, table, 0.0)
            rtab_ref[row:row + cells, at:at + 2 * cells] = part.astype(jnp.bfloat16)

    scale = 1.0 / math.sqrt(depth)
    ones = jnp.ones((columns - cells, nq * nr * cells), jnp.bfloat16)

    def correlate(t, v):
        block = lax.dot_general(qall[t], rall[v], (((1,), (1,)), ((), ())),
                                preferred_element_type=jnp.float32)
        block = (block * scale).astype(jnp.bfloat16)
        n = t * nw + v
        for p in range(nq):
            corr_ref[n, :cells, p * nr * cells:(p + 1) * nr * cells] = block[p * cells:(p + 1) * cells]
        corr_ref[n, cells:, :] = ones

    early = 3 if square else nb

    def at_distance(d):
        def one(m, carry):
            t, side = m // 4, m % 4
            if square:
                t = (by + t // 2) % 2 * 2 + (bx + t % 2) % 2
            if d == 0:
                @pl.when(side < 2)
                def _():
                    correlate(t, 2 * z + side)
            else:
                far = z + (side // 2 * 2 - 1) * d

                @pl.when((far >= 0) & (far <= last))
                def _():
                    correlate(t, 2 * far + side % 2)
            return carry
        lax.fori_loop(0, early * 4, one, 0)

    line_step(0)
    if square:
        for n in range(2):
            arrive[n].wait_recv()
            onward[n].start()
    if last > 1:
        line_step(1)
    if square:
        arrive[2].wait_recv()
        arrive[3].wait_recv()
    else:
        for c in arrive:
            c.wait_recv()
    hand(twin, 0).wait_recv()
    at_distance(0)
    for d in range(1, nz):
        if d > 2:
            line_step(d - 1)
        hand_step(d - 1)
        at_distance(d)
    if square:
        arrive[4].wait_recv()
        arrive[5].wait_recv()

        def rest(v, carry):
            correlate(across, v)
            return carry
        lax.fori_loop(0, nw, rest, 0)

    for c in small:
        c.wait()
    for c in first + onward:
        c.wait_send()
    hand(w, 0).wait_send()
    for s in range(last):
        @pl.when((z - s >= 0) & (z < last))
        def _():
            up(s).wait_send()

        @pl.when((z + s <= last) & (z > 0))
        def _():
            down(s).wait_send()

        @pl.when(z - 1 - s >= 0)
        def _():
            hand(w - 2 * s - 2, 1 + s).wait_send()

        @pl.when(z + 1 + s <= last)
        def _():
            hand(w + 2 * s + 2, nz + s).wait_send()


def score_kernel(nw, nb, nq, nr, cells, hid, cand_ref, corr_ref, qtab_ref, rtab_ref, out_ref,
                 hidden, filtered, items):
    b = lax.axis_index("blk")
    wide = 4 * cells
    out_ref[...] = jnp.zeros_like(out_ref)

    def scan(n, count):
        flag = cand_ref[n // nw, 0, n % nw] != 0

        @pl.when(flag)
        def _():
            items[count] = n
        return count + jnp.where(flag, 1, 0)

    count = lax.fori_loop(0, nb * nw, scan, jnp.int32(0))
    columns = out_ref.shape[2]
    halves = nq * nr // 4
    row_id = lax.broadcasted_iota(jnp.int32, (nq, columns), 0)
    lane_id = lax.broadcasted_iota(jnp.int32, (nq, columns), 1)
    left = lax.broadcasted_iota(jnp.int32, (cells, 2 * cells), 1) < cells
    left_row = lax.broadcasted_iota(jnp.int32, (1, 2 * cells), 1) < cells

    def members(i):
        return [items[jnp.clip(i * GROUP + g, 0, count - 1)] for g in range(GROUP)]

    def pool(own):
        for g in range(GROUP):
            t, v = own[g] // nw, own[g] % nw
            base = v * (nb * nr) + b * nr
            result = out_ref[t]
            for p in range(nq):
                row = (g * halves + p // 2) * cells
                lane = p % 2 * 2 * cells
                f = filtered[row:row + cells, lane:lane + 2 * cells]
                col = jnp.max(f, axis=0, keepdims=True)
                for r in range(2):
                    own_f = jnp.where(left if r == 0 else ~left, f, -jnp.inf)
                    own_c = jnp.where(left_row if r == 0 else ~left_row, col, 0.0)
                    total = (jnp.sum(jnp.max(own_f, axis=1, keepdims=True), axis=0, keepdims=True)
                             + jnp.sum(own_c, axis=1, keepdims=True))
                    total = total * (0.5 / cells)
                    result = jnp.where((row_id == p) & (lane_id == base + r), total, result)
            out_ref[t] = result

    filtered[...] = jnp.zeros_like(filtered)

    def group(i, carry):
        own = members(i)
        before = members(jnp.maximum(i - 1, 0))
        for g in range(GROUP):
            for h in range(halves):
                value = jnp.dot(qtab_ref[...], corr_ref[own[g], :, h * wide:(h + 1) * wide],
                                preferred_element_type=jnp.float32).astype(jnp.bfloat16)
                row = (g * halves + h) * cells
                for k in range(hid):
                    part = value[k * cells:(k + 1) * cells]
                    hidden[row:row + cells, k * wide:(k + 1) * wide] = jnp.maximum(part, jnp.bfloat16(0.0))
        pool(before)
        filtered[...] = jnp.dot(hidden[...], rtab_ref[...], preferred_element_type=jnp.float32)
        return carry

    groups = (count + GROUP - 1) // GROUP
    lax.fori_loop(0, groups, group, 0)

    @pl.when(count > 0)
    def _():
        pool(members(groups - 1))


def exchange_kernel(nw, nb, s_ref, out_ref, got, ss, sr):
    w, b = lax.axis_index("wide"), lax.axis_index("blk")
    barrier = pltpu.get_barrier_semaphore()
    for d in range(1, nb):
        pl.semaphore_signal(barrier, inc=1, device_id=(w, lax.rem(b + d, nb)), device_id_type=MESH)
    pl.semaphore_wait(barrier, nb - 1)
    copies = []
    for d in range(1, nb):
        to = lax.rem(b + d, nb)
        copies.append(pltpu.make_async_remote_copy(
            src_ref=s_ref.at[to], dst_ref=got.at[d], send_sem=ss.at[d], recv_sem=sr.at[d],
            device_id=(w, to), device_id_type=MESH))
    for c in copies:
        c.start()
    total = s_ref[b]
    for c in copies:
        c.wait()
    for d in range(1, nb):
        total = total + got[d]
    out_ref[...] = total


def shards(nw, nb, queries, references, query_taps, ref_taps, tap_bias, candidates):
    nq, cells, depth = queries.shape
    nr = references.shape[0]
    hid = query_taps.shape[0]
    dma = pltpu.SemaphoreType.DMA
    bf16 = jnp.bfloat16
    depth_in = cells + 16
    nz = nw // 2
    corr, qtab, rtab, cand = pl.pallas_call(
        functools.partial(gather_kernel, nw, nb),
        out_shape=(
            jax.ShapeDtypeStruct((nb * nw, depth_in, nq * nr * cells), bf16),
            jax.ShapeDtypeStruct((hid * cells, depth_in), bf16),
            jax.ShapeDtypeStruct((hid * 4 * cells, 4 * cells), bf16),
            jax.ShapeDtypeStruct((nb, 1, nw), jnp.int32),
        ),
        in_specs=[HBM] * 6,
        out_specs=(VMEM,) * 4,
        scratch_shapes=[
            pltpu.VMEM((nb, nq * cells, depth), bf16),
            pltpu.VMEM((nw, nr * cells, depth), bf16),
            pltpu.VMEM(queries.shape, bf16),
            pltpu.VMEM(references.shape, bf16),
            pltpu.VMEM(query_taps.shape, bf16),
            pltpu.VMEM(ref_taps.shape, bf16),
            pltpu.VMEM((1, hid), jnp.float32),
            dma((6,)), dma((max(nb, 6),)), dma((max(nb, 6),)), dma((2 * nz,)), dma((2 * nz,)),
            dma((2 * nz,)), dma((2 * nz,)), dma((nb,)), dma((nb,)),
        ],
        compiler_params=pltpu.CompilerParams(
            collective_id=0, has_side_effects=True, vmem_limit_bytes=40 * 2**20),
        name="gather",
    )(queries, references, query_taps, ref_taps, tap_bias.reshape(1, hid), candidates)
    rows = GROUP * nq * nr // 4 * cells
    scores = pl.pallas_call(
        functools.partial(score_kernel, nw, nb, nq, nr, cells, hid),
        out_shape=jax.ShapeDtypeStruct((nb, nq, nw * nb * nr), jnp.float32),
        in_specs=[SMEM, VMEM, VMEM, VMEM],
        out_specs=VMEM,
        scratch_shapes=[
            pltpu.VMEM((rows, hid * 4 * cells), bf16),
            pltpu.VMEM((rows, 4 * cells), jnp.float32),
            pltpu.SMEM((nb * nw,), jnp.int32),
        ],
        compiler_params=pltpu.CompilerParams(vmem_limit_bytes=40 * 2**20),
        name="score",
    )(cand, corr, qtab, rtab)
    return pl.pallas_call(
        functools.partial(exchange_kernel, nw, nb),
        out_shape=jax.ShapeDtypeStruct(scores.shape[1:], jnp.float32),
        in_specs=[VMEM],
        out_specs=VMEM,
        scratch_shapes=[pltpu.VMEM(scores.shape, jnp.float32), dma((nb,)), dma((nb,))],
        compiler_params=pltpu.CompilerParams(
            collective_id=1, has_side_effects=True, vmem_limit_bytes=16 * 2**20),
        name="exchange",
    )(scores)


def solution(mesh):
    nw, nb = mesh.shape["wide"], mesh.shape["blk"]
    placed = (
        P(("wide", "blk"), None, None),
        P(("wide", "blk"), None, None),
        P(),
        P(),
        P(),
        P(("wide", "blk"), None),
    )
    return jax.shard_map(
        functools.partial(shards, nw, nb), mesh=mesh, in_specs=placed,
        out_specs=P(("wide", "blk"), None), check_vma=False,
    )
```

```python
import functools
import math

import jax
import jax.numpy as jnp
from jax import lax
from jax.experimental import pallas as pl
from jax.experimental.pallas import tpu as pltpu
from jax.sharding import PartitionSpec as P

SIDE = 8
EPS = 1e-06
GROUP = 4
MESH = pl.DeviceIdType.MESH
VMEM = pl.BlockSpec(memory_space=pltpu.VMEM)
HBM = pl.BlockSpec(memory_space=pltpu.HBM)
SMEM = pl.BlockSpec(memory_space=pltpu.SMEM)


def normalize(values):
    values = values.astype(jnp.float32)
    inverse_rms = lax.rsqrt(jnp.mean(values * values, axis=-1, keepdims=True) + EPS)
    return (values * inverse_rms).astype(jnp.bfloat16)


def tap_masks(rows, lanes, outer_on_rows):
    row = lax.broadcasted_iota(jnp.int32, (rows, lanes), 0) % (SIDE * SIDE)
    lane = lax.broadcasted_iota(jnp.int32, (rows, lanes), 1) % (SIDE * SIDE)
    out_cell, in_cell = (row, lane) if outer_on_rows else (lane, row)
    dy = in_cell // SIDE - out_cell // SIDE
    dx = in_cell % SIDE - out_cell % SIDE
    return [(dy == t // 3 - 1) & (dx == t % 3 - 1) for t in range(9)]


def gather_kernel(nw, nb, q_hbm, r_hbm, qt_hbm, rt_hbm, bias_hbm, cand_hbm,
                  corr_ref, qtab_ref, rtab_ref, call_ref,
                  qall, rall, qin, rin, qt_in, rt_in, bias_in,
                  load, qs, qr, zs, zr, ss, sr, cs, cr):
    w, b = lax.axis_index("wide"), lax.axis_index("blk")
    nz = nw // 2
    z, core = w // 2, w % 2
    twin = w + 1 - 2 * core
    nq, cells, depth = q_hbm.shape
    nr = r_hbm.shape[0]
    hid = qt_hbm.shape[0]
    last = nz - 1

    loads = [pltpu.make_async_copy(src, dst, load.at[n]) for n, (src, dst) in enumerate((
        (r_hbm, rin), (q_hbm, qin), (cand_hbm, call_ref.at[b]),
        (qt_hbm, qt_in), (rt_hbm, rt_in), (bias_hbm, bias_in)))]
    for c in loads:
        c.start()

    def signal(where):
        pl.semaphore_signal(barrier, inc=1, device_id=where, device_id_type=MESH)

    barrier = pltpu.get_barrier_semaphore()
    for d in range(1, nb):
        signal((w, lax.rem(b + d, nb)))
    signal((twin, b))

    @pl.when(z > 0)
    def _():
        signal((w - 2, b))

    @pl.when(z < last)
    def _():
        signal((w + 2, b))

    loads[0].wait()
    rall[w] = normalize(rin[...]).reshape(nr * cells, depth)
    pl.semaphore_wait(barrier, nb + jnp.where(z > 0, 1, 0) + jnp.where(z < last, 1, 0))

    def remote(ref, send, recv, n, where):
        return pltpu.make_async_remote_copy(
            src_ref=ref, dst_ref=ref, send_sem=send.at[n], recv_sem=recv.at[n],
            device_id=where, device_id_type=MESH)

    def up(s):
        return remote(rall.at[w - 2 * s], zs, zr, s, (jnp.minimum(w + 2, nw - 2 + core), b))

    def up_in(s):
        return remote(rall.at[w - 2 * s - 2], zs, zr, s, (twin, b))

    def down(s):
        return remote(rall.at[w + 2 * s], zs, zr, nz + s, (jnp.maximum(w - 2, core), b))

    def down_in(s):
        return remote(rall.at[w + 2 * s + 2], zs, zr, nz + s, (twin, b))

    def hand(owner, n):
        return remote(rall.at[owner], ss, sr, n, (twin, b))

    def line_step(s):
        @pl.when(z - 1 - s >= 0)
        def _():
            up_in(s).wait_recv()
            if s + 1 < last:
                @pl.when(z < last)
                def _():
                    up(s + 1).start()
            hand(w - 2 * s - 2, 1 + s).start()

        @pl.when(z + 1 + s <= last)
        def _():
            down_in(s).wait_recv()
            if s + 1 < last:
                @pl.when(z > 0)
                def _():
                    down(s + 1).start()
            hand(w + 2 * s + 2, nz + s).start()

    def hand_step(s):
        @pl.when(z - 1 - s >= 0)
        def _():
            hand(twin - 2 * s - 2, 1 + s).wait_recv()

        @pl.when(z + 1 + s <= last)
        def _():
            hand(twin + 2 * s + 2, nz + s).wait_recv()

    square = nb == 4
    half = nq * cells // 2
    bx, by = b % 2, b // 2 % 2
    on_x, on_y, across = b + 1 - 2 * bx, b + 2 - 4 * by, nb - 1 - b

    def piece(owner, h, n, where):
        return remote(qall.at[owner, h * half:(h + 1) * half], qs, qr, n, (w, where))

    small = [remote(call_ref.at[b], cs, cr, d, (w, lax.rem(b + d, nb))) for d in range(1, nb)]
    if square:
        first = [piece(b, 0, 0, on_x), piece(b, 1, 2, on_y), piece(b, 1, 1, on_x), piece(b, 0, 3, on_y)]
        onward = [piece(on_x, 0, 4, on_y), piece(on_y, 1, 5, on_x)]
        arrive = [piece(on_x, 0, 0, on_x), piece(on_y, 1, 2, on_y), piece(on_x, 1, 1, on_x),
                  piece(on_y, 0, 3, on_y), piece(across, 0, 4, on_y), piece(across, 1, 5, on_x)]
    else:
        first = [remote(qall.at[b], qs, qr, d, (w, lax.rem(b + d, nb))) for d in range(1, nb)]
        onward = []
        arrive = [remote(qall.at[lax.rem(b + nb - d, nb)], qs, qr, d, (w, lax.rem(b + d, nb)))
                  for d in range(1, nb)]

    @pl.when(z < last)
    def _():
        up(0).start()

    @pl.when(z > 0)
    def _():
        down(0).start()

    loads[1].wait()
    qall[b] = normalize(qin[...]).reshape(nq * cells, depth)
    for c in first:
        c.start()
    hand(w, 0).start()
    for c in loads[2:]:
        c.wait()
    for c in small:
        c.start()

    lane = lax.broadcasted_iota(jnp.int32, (cells, 2 * cells), 1)
    left = lane < cells
    columns = qtab_ref.shape[1]
    taps = qt_in[...].astype(jnp.float32)
    bias = bias_in[...]
    masks = [m & left for m in tap_masks(cells, 2 * cells, True)]
    for k in range(hid):
        b0 = jnp.broadcast_to(bias[:, k:k + 1], (cells, 2 * cells))
        b1 = b0.astype(jnp.bfloat16).astype(jnp.float32)
        b2 = (b0 - b1).astype(jnp.bfloat16).astype(jnp.float32)
        b3 = b0 - b1 - b2
        table = jnp.where(lane == cells, b1, jnp.where(lane == cells + 1, b2, jnp.where(lane == cells + 2, b3, 0.0)))
        for t in range(9):
            table = jnp.where(masks[t], taps[k:k + 1, t:t + 1], table)
        qtab_ref[k * cells:(k + 1) * cells, :] = table.astype(jnp.bfloat16)[:, :columns]
    line_step(0)
    if square:
        for n in range(2):
            arrive[n].wait_recv()
            onward[n].start()
    if last > 1:
        line_step(1)
    taps = rt_in[...].astype(jnp.float32)
    masks = tap_masks(cells, 2 * cells, False)
    rtab_ref[...] = jnp.zeros_like(rtab_ref)
    for k in range(hid):
        table = jnp.zeros((cells, 2 * cells), jnp.float32)
        for t in range(9):
            table = jnp.where(masks[t], taps[k:k + 1, t:t + 1], table)
        for s in range(4):
            row = (k * 4 + s) * cells
            at = s // 2 * 2 * cells
            part = jnp.where(left if s % 2 == 0 else ~left, table, 0.0)
            rtab_ref[row:row + cells, at:at + 2 * cells] = part.astype(jnp.bfloat16)

    scale = 1.0 / math.sqrt(depth)
    ones = jnp.ones((columns - cells, nq * nr * cells), jnp.bfloat16)

    def correlate(t, v):
        block = lax.dot_general(qall[t], rall[v], (((1,), (1,)), ((), ())),
                                preferred_element_type=jnp.float32)
        block = (block * scale).astype(jnp.bfloat16)
        n = t * nw + v
        for p in range(nq):
            corr_ref[n, :cells, p * nr * cells:(p + 1) * nr * cells] = block[p * cells:(p + 1) * cells]
        corr_ref[n, cells:, :] = ones

    early = 3 if square else nb

    def at_distance(d):
        def one(m, carry):
            t, side = m // 4, m % 4
            if square:
                t = (by + t // 2) % 2 * 2 + (bx + t % 2) % 2
            if d == 0:
                @pl.when(side < 2)
                def _():
                    correlate(t, 2 * z + side)
            else:
                far = z + (side // 2 * 2 - 1) * d

                @pl.when((far >= 0) & (far <= last))
                def _():
                    correlate(t, 2 * far + side % 2)
            return carry
        lax.fori_loop(0, early * 4, one, 0)

    if square:
        arrive[2].wait_recv()
        arrive[3].wait_recv()
    else:
        for c in arrive:
            c.wait_recv()
    hand(twin, 0).wait_recv()
    at_distance(0)
    for d in range(1, nz):
        if d > 2:
            line_step(d - 1)
        hand_step(d - 1)
        at_distance(d)
    if square:
        arrive[4].wait_recv()
        arrive[5].wait_recv()

        def rest(v, carry):
            correlate(across, v)
            return carry
        lax.fori_loop(0, nw, rest, 0)

    for c in small:
        c.wait()
    for c in first + onward:
        c.wait_send()
    hand(w, 0).wait_send()
    for s in range(last):
        @pl.when((z - s >= 0) & (z < last))
        def _():
            up(s).wait_send()

        @pl.when((z + s <= last) & (z > 0))
        def _():
            down(s).wait_send()

        @pl.when(z - 1 - s >= 0)
        def _():
            hand(w - 2 * s - 2, 1 + s).wait_send()

        @pl.when(z + 1 + s <= last)
        def _():
            hand(w + 2 * s + 2, nz + s).wait_send()


def score_kernel(nw, nb, nq, nr, cells, hid, cand_ref, corr_ref, qtab_ref, rtab_ref, out_ref,
                 hidden, filtered, items):
    b = lax.axis_index("blk")
    wide = 4 * cells
    out_ref[...] = jnp.zeros_like(out_ref)

    def scan(n, count):
        flag = cand_ref[n // nw, 0, n % nw] != 0

        @pl.when(flag)
        def _():
            items[count] = n
        return count + jnp.where(flag, 1, 0)

    count = lax.fori_loop(0, nb * nw, scan, jnp.int32(0))
    columns = out_ref.shape[2]
    halves = nq * nr // 4
    row_id = lax.broadcasted_iota(jnp.int32, (nq, columns), 0)
    lane_id = lax.broadcasted_iota(jnp.int32, (nq, columns), 1)
    left = lax.broadcasted_iota(jnp.int32, (cells, 2 * cells), 1) < cells
    left_row = lax.broadcasted_iota(jnp.int32, (1, 2 * cells), 1) < cells

    def members(i, size):
        return [items[jnp.maximum(i, 0) * GROUP + g] for g in range(size)]

    def pool(own):
        for g in range(len(own)):
            t, v = own[g] // nw, own[g] % nw
            base = v * (nb * nr) + b * nr
            result = out_ref[t]
            for p in range(nq):
                row = (g * halves + p // 2) * cells
                lane = p % 2 * 2 * cells
                f = filtered[row:row + cells, lane:lane + 2 * cells]
                col = jnp.max(f, axis=0, keepdims=True)
                for r in range(2):
                    own_f = jnp.where(left if r == 0 else ~left, f, -jnp.inf)
                    own_c = jnp.where(left_row if r == 0 else ~left_row, col, 0.0)
                    total = (jnp.sum(jnp.max(own_f, axis=1, keepdims=True), axis=0, keepdims=True)
                             + jnp.sum(own_c, axis=1, keepdims=True))
                    total = total * (0.5 / cells)
                    result = jnp.where((row_id == p) & (lane_id == base + r), total, result)
            out_ref[t] = result

    filtered[...] = jnp.zeros_like(filtered)

    def group(i, size, before):
        own = members(i, size)
        for g in range(size):
            for h in range(halves):
                value = jnp.dot(qtab_ref[...], corr_ref[own[g], :, h * wide:(h + 1) * wide],
                                preferred_element_type=jnp.float32).astype(jnp.bfloat16)
                row = (g * halves + h) * cells
                for k in range(hid):
                    part = value[k * cells:(k + 1) * cells]
                    hidden[row:row + cells, k * wide:(k + 1) * wide] = jnp.maximum(part, jnp.bfloat16(0.0))
        pool(before)
        rows = size * halves * cells
        filtered[:rows, :] = jnp.dot(hidden[:rows, :], rtab_ref[...], preferred_element_type=jnp.float32)

    def whole_group(i, carry):
        group(i, GROUP, members(i - 1, GROUP))
        return carry

    groups = count // GROUP
    left_over = count - groups * GROUP
    lax.fori_loop(0, groups, whole_group, 0)

    @pl.when((left_over == 0) & (groups > 0))
    def _():
        pool(members(groups - 1, GROUP))

    for size in range(1, GROUP):
        @pl.when((left_over == size) & (groups > 0))
        def _():
            group(groups, size, members(groups - 1, GROUP))
            pool(members(groups, size))

    for size in range(1, GROUP):
        @pl.when((left_over == size) & (groups == 0))
        def _():
            group(groups, size, [])
            pool(members(groups, size))


def exchange_kernel(nw, nb, s_ref, out_ref, got, ss, sr):
    w, b = lax.axis_index("wide"), lax.axis_index("blk")
    barrier = pltpu.get_barrier_semaphore()
    for d in range(1, nb):
        pl.semaphore_signal(barrier, inc=1, device_id=(w, lax.rem(b + d, nb)), device_id_type=MESH)
    pl.semaphore_wait(barrier, nb - 1)
    copies = []
    for d in range(1, nb):
        to = lax.rem(b + d, nb)
        copies.append(pltpu.make_async_remote_copy(
            src_ref=s_ref.at[to], dst_ref=got.at[d], send_sem=ss.at[d], recv_sem=sr.at[d],
            device_id=(w, to), device_id_type=MESH))
    for c in copies:
        c.start()
    total = s_ref[b]
    for c in copies:
        c.wait()
    for d in range(1, nb):
        total = total + got[d]
    out_ref[...] = total


def shards(nw, nb, queries, references, query_taps, ref_taps, tap_bias, candidates):
    nq, cells, depth = queries.shape
    nr = references.shape[0]
    hid = query_taps.shape[0]
    dma = pltpu.SemaphoreType.DMA
    bf16 = jnp.bfloat16
    depth_in = cells + 16
    nz = nw // 2
    corr, qtab, rtab, cand = pl.pallas_call(
        functools.partial(gather_kernel, nw, nb),
        out_shape=(
            jax.ShapeDtypeStruct((nb * nw, depth_in, nq * nr * cells), bf16),
            jax.ShapeDtypeStruct((hid * cells, depth_in), bf16),
            jax.ShapeDtypeStruct((hid * 4 * cells, 4 * cells), bf16),
            jax.ShapeDtypeStruct((nb, 1, nw), jnp.int32),
        ),
        in_specs=[HBM] * 6,
        out_specs=(VMEM,) * 4,
        scratch_shapes=[
            pltpu.VMEM((nb, nq * cells, depth), bf16),
            pltpu.VMEM((nw, nr * cells, depth), bf16),
            pltpu.VMEM(queries.shape, bf16),
            pltpu.VMEM(references.shape, bf16),
            pltpu.VMEM(query_taps.shape, bf16),
            pltpu.VMEM(ref_taps.shape, bf16),
            pltpu.VMEM((1, hid), jnp.float32),
            dma((6,)), dma((max(nb, 6),)), dma((max(nb, 6),)), dma((2 * nz,)), dma((2 * nz,)),
            dma((2 * nz,)), dma((2 * nz,)), dma((nb,)), dma((nb,)),
        ],
        compiler_params=pltpu.CompilerParams(
            collective_id=0, has_side_effects=True, vmem_limit_bytes=40 * 2**20),
        name="gather",
    )(queries, references, query_taps, ref_taps, tap_bias.reshape(1, hid), candidates)
    rows = GROUP * nq * nr // 4 * cells
    scores = pl.pallas_call(
        functools.partial(score_kernel, nw, nb, nq, nr, cells, hid),
        out_shape=jax.ShapeDtypeStruct((nb, nq, nw * nb * nr), jnp.float32),
        in_specs=[SMEM, VMEM, VMEM, VMEM],
        out_specs=VMEM,
        scratch_shapes=[
            pltpu.VMEM((rows, hid * 4 * cells), bf16),
            pltpu.VMEM((rows, 4 * cells), jnp.float32),
            pltpu.SMEM((nb * nw,), jnp.int32),
        ],
        compiler_params=pltpu.CompilerParams(vmem_limit_bytes=40 * 2**20),
        name="score",
    )(cand, corr, qtab, rtab)
    return pl.pallas_call(
        functools.partial(exchange_kernel, nw, nb),
        out_shape=jax.ShapeDtypeStruct(scores.shape[1:], jnp.float32),
        in_specs=[VMEM],
        out_specs=VMEM,
        scratch_shapes=[pltpu.VMEM(scores.shape, jnp.float32), dma((nb,)), dma((nb,))],
        compiler_params=pltpu.CompilerParams(
            collective_id=1, has_side_effects=True, vmem_limit_bytes=16 * 2**20),
        name="exchange",
    )(scores)


def solution(mesh):
    nw, nb = mesh.shape["wide"], mesh.shape["blk"]
    placed = (
        P(("wide", "blk"), None, None),
        P(("wide", "blk"), None, None),
        P(),
        P(),
        P(),
        P(("wide", "blk"), None),
    )
    return jax.shard_map(
        functools.partial(shards, nw, nb), mesh=mesh, in_specs=placed,
        out_specs=P(("wide", "blk"), None), check_vma=False,
    )
```

```python
import functools
import math

import jax
import jax.numpy as jnp
from jax import lax
from jax.experimental import pallas as pl
from jax.experimental.pallas import tpu as pltpu
from jax.sharding import PartitionSpec as P

SIDE = 8
EPS = 1e-06
GROUP = 4
MESH = pl.DeviceIdType.MESH
VMEM = pl.BlockSpec(memory_space=pltpu.VMEM)
HBM = pl.BlockSpec(memory_space=pltpu.HBM)
SMEM = pl.BlockSpec(memory_space=pltpu.SMEM)


def normalize(values):
    values = values.astype(jnp.float32)
    inverse_rms = lax.rsqrt(jnp.mean(values * values, axis=-1, keepdims=True) + EPS)
    return (values * inverse_rms).astype(jnp.bfloat16)


def tap_masks(rows, lanes, outer_on_rows):
    row = lax.broadcasted_iota(jnp.int32, (rows, lanes), 0) % (SIDE * SIDE)
    lane = lax.broadcasted_iota(jnp.int32, (rows, lanes), 1) % (SIDE * SIDE)
    out_cell, in_cell = (row, lane) if outer_on_rows else (lane, row)
    dy = in_cell // SIDE - out_cell // SIDE
    dx = in_cell % SIDE - out_cell % SIDE
    return [(dy == t // 3 - 1) & (dx == t % 3 - 1) for t in range(9)]


def gather_kernel(nw, nb, q_hbm, r_hbm, qt_hbm, rt_hbm, bias_hbm, cand_hbm,
                  corr_hbm, qtab_hbm, rtab_hbm, call_ref,
                  corr_ref, qtab_ref, rtab_ref, store, qall, rall, qin, rin, qt_in, rt_in, bias_in,
                  load, qs, qr, zs, zr, ss, sr, cs, cr):
    w, b = lax.axis_index("wide"), lax.axis_index("blk")
    nz = nw // 2
    z, core = w // 2, w % 2
    twin = w + 1 - 2 * core
    nq, cells, depth = q_hbm.shape
    nr = r_hbm.shape[0]
    hid = qt_hbm.shape[0]
    last = nz - 1

    loads = [pltpu.make_async_copy(src, dst, load.at[n]) for n, (src, dst) in enumerate((
        (r_hbm, rin), (q_hbm, qin), (cand_hbm, call_ref.at[b]),
        (qt_hbm, qt_in), (rt_hbm, rt_in), (bias_hbm, bias_in)))]
    for c in loads:
        c.start()

    def signal(where):
        pl.semaphore_signal(barrier, inc=1, device_id=where, device_id_type=MESH)

    barrier = pltpu.get_barrier_semaphore()
    for d in range(1, nb):
        signal((w, lax.rem(b + d, nb)))
    signal((twin, b))

    @pl.when(z > 0)
    def _():
        signal((w - 2, b))

    @pl.when(z < last)
    def _():
        signal((w + 2, b))

    loads[0].wait()
    rall[w] = normalize(rin[...]).reshape(nr * cells, depth)
    pl.semaphore_wait(barrier, nb + jnp.where(z > 0, 1, 0) + jnp.where(z < last, 1, 0))

    def remote(ref, send, recv, n, where):
        return pltpu.make_async_remote_copy(
            src_ref=ref, dst_ref=ref, send_sem=send.at[n], recv_sem=recv.at[n],
            device_id=where, device_id_type=MESH)

    def up(s):
        return remote(rall.at[w - 2 * s], zs, zr, s, (jnp.minimum(w + 2, nw - 2 + core), b))

    def up_in(s):
        return remote(rall.at[w - 2 * s - 2], zs, zr, s, (twin, b))

    def down(s):
        return remote(rall.at[w + 2 * s], zs, zr, nz + s, (jnp.maximum(w - 2, core), b))

    def down_in(s):
        return remote(rall.at[w + 2 * s + 2], zs, zr, nz + s, (twin, b))

    def hand(owner, n):
        return remote(rall.at[owner], ss, sr, n, (twin, b))

    def line_step(s):
        @pl.when(z - 1 - s >= 0)
        def _():
            up_in(s).wait_recv()
            if s + 1 < last:
                @pl.when(z < last)
                def _():
                    up(s + 1).start()
            hand(w - 2 * s - 2, 1 + s).start()

        @pl.when(z + 1 + s <= last)
        def _():
            down_in(s).wait_recv()
            if s + 1 < last:
                @pl.when(z > 0)
                def _():
                    down(s + 1).start()
            hand(w + 2 * s + 2, nz + s).start()

    def hand_step(s):
        @pl.when(z - 1 - s >= 0)
        def _():
            hand(twin - 2 * s - 2, 1 + s).wait_recv()

        @pl.when(z + 1 + s <= last)
        def _():
            hand(twin + 2 * s + 2, nz + s).wait_recv()

    square = nb == 4
    half = nq * cells // 2
    bx, by = b % 2, b // 2 % 2
    on_x, on_y, across = b + 1 - 2 * bx, b + 2 - 4 * by, nb - 1 - b

    def piece(owner, h, n, where):
        return remote(qall.at[owner, h * half:(h + 1) * half], qs, qr, n, (w, where))

    small = [remote(call_ref.at[b], cs, cr, d, (w, lax.rem(b + d, nb))) for d in range(1, nb)]
    if square:
        first = [piece(b, 0, 0, on_x), piece(b, 1, 2, on_y), piece(b, 1, 1, on_x), piece(b, 0, 3, on_y)]
        onward = [piece(on_x, 0, 4, on_y), piece(on_y, 1, 5, on_x)]
        arrive = [piece(on_x, 0, 0, on_x), piece(on_y, 1, 2, on_y), piece(on_x, 1, 1, on_x),
                  piece(on_y, 0, 3, on_y), piece(across, 0, 4, on_y), piece(across, 1, 5, on_x)]
    else:
        first = [remote(qall.at[b], qs, qr, d, (w, lax.rem(b + d, nb))) for d in range(1, nb)]
        onward = []
        arrive = [remote(qall.at[lax.rem(b + nb - d, nb)], qs, qr, d, (w, lax.rem(b + d, nb)))
                  for d in range(1, nb)]

    @pl.when(z < last)
    def _():
        up(0).start()

    @pl.when(z > 0)
    def _():
        down(0).start()

    loads[1].wait()
    qall[b] = normalize(qin[...]).reshape(nq * cells, depth)
    for c in first:
        c.start()
    hand(w, 0).start()
    for c in loads[2:]:
        c.wait()
    for c in small:
        c.start()

    lane = lax.broadcasted_iota(jnp.int32, (cells, 2 * cells), 1)
    left = lane < cells
    columns = qtab_ref.shape[1]
    taps = qt_in[...].astype(jnp.float32)
    bias = bias_in[...]
    masks = [m & left for m in tap_masks(cells, 2 * cells, True)]
    for k in range(hid):
        b0 = jnp.broadcast_to(bias[:, k:k + 1], (cells, 2 * cells))
        b1 = b0.astype(jnp.bfloat16).astype(jnp.float32)
        b2 = (b0 - b1).astype(jnp.bfloat16).astype(jnp.float32)
        b3 = b0 - b1 - b2
        table = jnp.where(lane == cells, b1, jnp.where(lane == cells + 1, b2, jnp.where(lane == cells + 2, b3, 0.0)))
        for t in range(9):
            table = jnp.where(masks[t], taps[k:k + 1, t:t + 1], table)
        qtab_ref[k * cells:(k + 1) * cells, :] = table.astype(jnp.bfloat16)[:, :columns]
    line_step(0)
    if square:
        for n in range(2):
            arrive[n].wait_recv()
            onward[n].start()
    if last > 1:
        line_step(1)
    taps = rt_in[...].astype(jnp.float32)
    masks = tap_masks(cells, 2 * cells, False)
    rtab_ref[...] = jnp.zeros_like(rtab_ref)
    for k in range(hid):
        table = jnp.zeros((cells, 2 * cells), jnp.float32)
        for t in range(9):
            table = jnp.where(masks[t], taps[k:k + 1, t:t + 1], table)
        for s in range(4):
            row = (k * 4 + s) * cells
            at = s // 2 * 2 * cells
            part = jnp.where(left if s % 2 == 0 else ~left, table, 0.0)
            rtab_ref[row:row + cells, at:at + 2 * cells] = part.astype(jnp.bfloat16)

    tables = [pltpu.make_async_copy(qtab_ref, qtab_hbm, store.at[nb * nz]),
              pltpu.make_async_copy(rtab_ref, rtab_hbm, store.at[nb * nz + 1])]
    for c in tables:
        c.start()
    scale = 1.0 / math.sqrt(depth)
    ones = jnp.ones((columns - cells, nq * nr * cells), jnp.bfloat16)

    def leave(t, far):
        at = pl.ds(t * nw + 2 * far, 2)
        return pltpu.make_async_copy(corr_ref.at[at], corr_hbm.at[at], store.at[t * nz + far])

    def correlate(t, far):
        pair = rall[pl.ds(2 * far, 2)].reshape(2 * nr * cells, depth)
        block = lax.dot_general(qall[t], pair, (((1,), (1,)), ((), ())),
                                preferred_element_type=jnp.float32)
        block = (block * scale).astype(jnp.bfloat16)
        for side in range(2):
            n = t * nw + 2 * far + side
            lanes = slice(side * nr * cells, (side + 1) * nr * cells)
            for p in range(nq):
                corr_ref[n, :cells, p * nr * cells:(p + 1) * nr * cells] = block[p * cells:(p + 1) * cells, lanes]
            corr_ref[n, cells:, :] = ones
        leave(t, far).start()

    early = 3 if square else nb

    def at_distance(d):
        def one(m, carry):
            t, side = m // 2, m % 2
            if square:
                t = (by + t // 2) % 2 * 2 + (bx + t % 2) % 2
            far = z + (side * 2 - 1) * d

            @pl.when((far >= 0) & (far <= last))
            def _():
                correlate(t, far)
            return carry

        def here(m, carry):
            if square:
                m = (by + m // 2) % 2 * 2 + (bx + m % 2) % 2
            correlate(m, z)
            return carry

        if d == 0:
            lax.fori_loop(0, early, here, 0)
        else:
            lax.fori_loop(0, early * 2, one, 0)

    if square:
        arrive[2].wait_recv()
        arrive[3].wait_recv()
    else:
        for c in arrive:
            c.wait_recv()
    hand(twin, 0).wait_recv()
    at_distance(0)
    for d in range(1, nz):
        if d > 2:
            line_step(d - 1)
        hand_step(d - 1)
        at_distance(d)
    if square:
        arrive[4].wait_recv()
        arrive[5].wait_recv()

        def rest(far, carry):
            correlate(across, far)
            return carry
        lax.fori_loop(0, nz, rest, 0)

    for c in small + tables:
        c.wait()
    for c in first + onward:
        c.wait_send()
    hand(w, 0).wait_send()
    for s in range(last):
        @pl.when((z - s >= 0) & (z < last))
        def _():
            up(s).wait_send()

        @pl.when((z + s <= last) & (z > 0))
        def _():
            down(s).wait_send()

        @pl.when(z - 1 - s >= 0)
        def _():
            hand(w - 2 * s - 2, 1 + s).wait_send()

        @pl.when(z + 1 + s <= last)
        def _():
            hand(w + 2 * s + 2, nz + s).wait_send()

    def left_for(n, carry):
        leave(n // nz, n % nz).wait()
        return carry
    lax.fori_loop(0, nb * nz, left_for, 0)


def score_kernel(nw, nb, nq, nr, cells, hid, cand_ref, corr_hbm, qtab_hbm, rtab_hbm, out_ref,
                 corr_ref, qtab_ref, rtab_ref, load, hidden, filtered, items):
    b = lax.axis_index("blk")
    wide = 4 * cells
    loads = [pltpu.make_async_copy(src, dst, load.at[n]) for n, (src, dst) in enumerate((
        (qtab_hbm, qtab_ref), (corr_hbm, corr_ref), (rtab_hbm, rtab_ref)))]
    for c in loads:
        c.start()
    out_ref[...] = jnp.zeros_like(out_ref)

    def scan(n, count):
        flag = cand_ref[n // nw, 0, n % nw] != 0

        @pl.when(flag)
        def _():
            items[count] = n
        return count + jnp.where(flag, 1, 0)

    count = lax.fori_loop(0, nb * nw, scan, jnp.int32(0))
    columns = out_ref.shape[2]
    halves = nq * nr // 4
    row_id = lax.broadcasted_iota(jnp.int32, (nq, columns), 0)
    lane_id = lax.broadcasted_iota(jnp.int32, (nq, columns), 1)
    left = lax.broadcasted_iota(jnp.int32, (cells, 2 * cells), 1) < cells
    left_row = lax.broadcasted_iota(jnp.int32, (1, 2 * cells), 1) < cells

    def members(i, size):
        return [items[jnp.maximum(i, 0) * GROUP + g] for g in range(size)]

    def pool(own):
        for g in range(len(own)):
            t, v = own[g] // nw, own[g] % nw
            base = v * (nb * nr) + b * nr
            result = out_ref[t]
            for p in range(nq):
                row = (g * halves + p // 2) * cells
                lane = p % 2 * 2 * cells
                f = filtered[row:row + cells, lane:lane + 2 * cells]
                col = jnp.max(f, axis=0, keepdims=True)
                for r in range(2):
                    own_f = jnp.where(left if r == 0 else ~left, f, -jnp.inf)
                    own_c = jnp.where(left_row if r == 0 else ~left_row, col, 0.0)
                    total = (jnp.sum(jnp.max(own_f, axis=1, keepdims=True), axis=0, keepdims=True)
                             + jnp.sum(own_c, axis=1, keepdims=True))
                    total = total * (0.5 / cells)
                    result = jnp.where((row_id == p) & (lane_id == base + r), total, result)
            out_ref[t] = result

    filtered[...] = jnp.zeros_like(filtered)

    def group(i, size, before):
        own = members(i, size)
        for g in range(size):
            for h in range(halves):
                value = jnp.dot(qtab_ref[...], corr_ref[own[g], :, h * wide:(h + 1) * wide],
                                preferred_element_type=jnp.float32).astype(jnp.bfloat16)
                row = (g * halves + h) * cells
                for k in range(hid):
                    part = value[k * cells:(k + 1) * cells]
                    hidden[row:row + cells, k * wide:(k + 1) * wide] = jnp.maximum(part, jnp.bfloat16(0.0))
        pool(before)
        rows = size * halves * cells
        filtered[:rows, :] = jnp.dot(hidden[:rows, :], rtab_ref[...], preferred_element_type=jnp.float32)

    def whole_group(i, carry):
        group(i, GROUP, members(i - 1, GROUP))
        return carry

    for c in loads:
        c.wait()
    groups = count // GROUP
    left_over = count - groups * GROUP
    lax.fori_loop(0, groups, whole_group, 0)

    @pl.when((left_over == 0) & (groups > 0))
    def _():
        pool(members(groups - 1, GROUP))

    for size in range(1, GROUP):
        @pl.when((left_over == size) & (groups > 0))
        def _():
            group(groups, size, members(groups - 1, GROUP))
            pool(members(groups, size))

    for size in range(1, GROUP):
        @pl.when((left_over == size) & (groups == 0))
        def _():
            group(groups, size, [])
            pool(members(groups, size))


def exchange_kernel(nw, nb, s_ref, out_ref, got, ss, sr):
    w, b = lax.axis_index("wide"), lax.axis_index("blk")
    barrier = pltpu.get_barrier_semaphore()
    for d in range(1, nb):
        pl.semaphore_signal(barrier, inc=1, device_id=(w, lax.rem(b + d, nb)), device_id_type=MESH)
    pl.semaphore_wait(barrier, nb - 1)
    copies = []
    for d in range(1, nb):
        to = lax.rem(b + d, nb)
        copies.append(pltpu.make_async_remote_copy(
            src_ref=s_ref.at[to], dst_ref=got.at[d], send_sem=ss.at[d], recv_sem=sr.at[d],
            device_id=(w, to), device_id_type=MESH))
    for c in copies:
        c.start()
    total = s_ref[b]
    for c in copies:
        c.wait()
    for d in range(1, nb):
        total = total + got[d]
    out_ref[...] = total


def shards(nw, nb, queries, references, query_taps, ref_taps, tap_bias, candidates):
    nq, cells, depth = queries.shape
    nr = references.shape[0]
    hid = query_taps.shape[0]
    dma = pltpu.SemaphoreType.DMA
    bf16 = jnp.bfloat16
    depth_in = cells + 16
    nz = nw // 2
    corr, qtab, rtab, cand = pl.pallas_call(
        functools.partial(gather_kernel, nw, nb),
        out_shape=(
            jax.ShapeDtypeStruct((nb * nw, depth_in, nq * nr * cells), bf16),
            jax.ShapeDtypeStruct((hid * cells, depth_in), bf16),
            jax.ShapeDtypeStruct((hid * 4 * cells, 4 * cells), bf16),
            jax.ShapeDtypeStruct((nb, 1, nw), jnp.int32),
        ),
        in_specs=[HBM] * 6,
        out_specs=(HBM, HBM, HBM, VMEM),
        scratch_shapes=[
            pltpu.VMEM((nb * nw, depth_in, nq * nr * cells), bf16),
            pltpu.VMEM((hid * cells, depth_in), bf16),
            pltpu.VMEM((hid * 4 * cells, 4 * cells), bf16),
            dma((nb * nz + 2,)),
            pltpu.VMEM((nb, nq * cells, depth), bf16),
            pltpu.VMEM((nw, nr * cells, depth), bf16),
            pltpu.VMEM(queries.shape, bf16),
            pltpu.VMEM(references.shape, bf16),
            pltpu.VMEM(query_taps.shape, bf16),
            pltpu.VMEM(ref_taps.shape, bf16),
            pltpu.VMEM((1, hid), jnp.float32),
            dma((6,)), dma((max(nb, 6),)), dma((max(nb, 6),)), dma((2 * nz,)), dma((2 * nz,)),
            dma((2 * nz,)), dma((2 * nz,)), dma((nb,)), dma((nb,)),
        ],
        compiler_params=pltpu.CompilerParams(
            collective_id=0, has_side_effects=True, vmem_limit_bytes=56 * 2**20),
        name="gather",
    )(queries, references, query_taps, ref_taps, tap_bias.reshape(1, hid), candidates)
    rows = GROUP * nq * nr // 4 * cells
    scores = pl.pallas_call(
        functools.partial(score_kernel, nw, nb, nq, nr, cells, hid),
        out_shape=jax.ShapeDtypeStruct((nb, nq, nw * nb * nr), jnp.float32),
        in_specs=[SMEM, HBM, HBM, HBM],
        out_specs=VMEM,
        scratch_shapes=[
            pltpu.VMEM(corr.shape, bf16),
            pltpu.VMEM(qtab.shape, bf16),
            pltpu.VMEM(rtab.shape, bf16),
            dma((3,)),
            pltpu.VMEM((rows, hid * 4 * cells), bf16),
            pltpu.VMEM((rows, 4 * cells), jnp.float32),
            pltpu.SMEM((nb * nw,), jnp.int32),
        ],
        compiler_params=pltpu.CompilerParams(vmem_limit_bytes=56 * 2**20),
        name="score",
    )(cand, corr, qtab, rtab)
    return pl.pallas_call(
        functools.partial(exchange_kernel, nw, nb),
        out_shape=jax.ShapeDtypeStruct(scores.shape[1:], jnp.float32),
        in_specs=[VMEM],
        out_specs=VMEM,
        scratch_shapes=[pltpu.VMEM(scores.shape, jnp.float32), dma((nb,)), dma((nb,))],
        compiler_params=pltpu.CompilerParams(
            collective_id=1, has_side_effects=True, vmem_limit_bytes=16 * 2**20),
        name="exchange",
    )(scores)


def solution(mesh):
    nw, nb = mesh.shape["wide"], mesh.shape["blk"]
    placed = (
        P(("wide", "blk"), None, None),
        P(("wide", "blk"), None, None),
        P(),
        P(),
        P(),
        P(("wide", "blk"), None),
    )
    return jax.shard_map(
        functools.partial(shards, nw, nb), mesh=mesh, in_specs=placed,
        out_specs=P(("wide", "blk"), None), check_vma=False,
    )
```

```python
import functools
import math

import jax
import jax.numpy as jnp
from jax import lax
from jax.experimental import pallas as pl
from jax.experimental.pallas import tpu as pltpu
from jax.sharding import PartitionSpec as P

SIDE = 8
EPS = 1e-06
GROUP = 4
MESH = pl.DeviceIdType.MESH
VMEM = pl.BlockSpec(memory_space=pltpu.VMEM)
HBM = pl.BlockSpec(memory_space=pltpu.HBM)
SMEM = pl.BlockSpec(memory_space=pltpu.SMEM)


def normalize(values):
    values = values.astype(jnp.float32)
    inverse_rms = lax.rsqrt(jnp.mean(values * values, axis=-1, keepdims=True) + EPS)
    return (values * inverse_rms).astype(jnp.bfloat16)


def tap_masks(rows, lanes, outer_on_rows):
    row = lax.broadcasted_iota(jnp.int32, (rows, lanes), 0) % (SIDE * SIDE)
    lane = lax.broadcasted_iota(jnp.int32, (rows, lanes), 1) % (SIDE * SIDE)
    out_cell, in_cell = (row, lane) if outer_on_rows else (lane, row)
    dy = in_cell // SIDE - out_cell // SIDE
    dx = in_cell % SIDE - out_cell % SIDE
    return [(dy == t // 3 - 1) & (dx == t % 3 - 1) for t in range(9)]


def gather_kernel(nw, nb, q_hbm, r_hbm, qt_hbm, rt_hbm, bias_hbm, cand_hbm,
                  corr_hbm, qtab_hbm, rtab_hbm, call_ref,
                  corr_ref, qtab_ref, rtab_ref, store, qall, rall, qin, rin, qt_in, rt_in, bias_in,
                  load, qs, qr, zs, zr, ss, sr, cs, cr):
    w, b = lax.axis_index("wide"), lax.axis_index("blk")
    nz = nw // 2
    z, core = w // 2, w % 2
    twin = w + 1 - 2 * core
    nq, cells, depth = q_hbm.shape
    nr = r_hbm.shape[0]
    hid = qt_hbm.shape[0]
    last = nz - 1

    loads = [pltpu.make_async_copy(src, dst, load.at[n]) for n, (src, dst) in enumerate((
        (r_hbm, rin), (q_hbm, qin), (cand_hbm, call_ref.at[b]),
        (qt_hbm, qt_in), (rt_hbm, rt_in), (bias_hbm, bias_in)))]
    for c in loads:
        c.start()

    def signal(where):
        pl.semaphore_signal(barrier, inc=1, device_id=where, device_id_type=MESH)

    barrier = pltpu.get_barrier_semaphore()
    for d in range(1, nb):
        signal((w, lax.rem(b + d, nb)))
    signal((twin, b))

    @pl.when(z > 0)
    def _():
        signal((w - 2, b))

    @pl.when(z < last)
    def _():
        signal((w + 2, b))

    loads[0].wait()
    rall[w] = normalize(rin[...]).reshape(nr * cells, depth)
    pl.semaphore_wait(barrier, nb + jnp.where(z > 0, 1, 0) + jnp.where(z < last, 1, 0))

    def remote(ref, send, recv, n, where):
        return pltpu.make_async_remote_copy(
            src_ref=ref, dst_ref=ref, send_sem=send.at[n], recv_sem=recv.at[n],
            device_id=where, device_id_type=MESH)

    def up(s):
        return remote(rall.at[w - 2 * s], zs, zr, s, (jnp.minimum(w + 2, nw - 2 + core), b))

    def up_in(s):
        return remote(rall.at[w - 2 * s - 2], zs, zr, s, (twin, b))

    def down(s):
        return remote(rall.at[w + 2 * s], zs, zr, nz + s, (jnp.maximum(w - 2, core), b))

    def down_in(s):
        return remote(rall.at[w + 2 * s + 2], zs, zr, nz + s, (twin, b))

    def hand(owner, n):
        return remote(rall.at[owner], ss, sr, n, (twin, b))

    def line_step(s):
        @pl.when(z - 1 - s >= 0)
        def _():
            up_in(s).wait_recv()
            if s + 1 < last:
                @pl.when(z < last)
                def _():
                    up(s + 1).start()
            hand(w - 2 * s - 2, 1 + s).start()

        @pl.when(z + 1 + s <= last)
        def _():
            down_in(s).wait_recv()
            if s + 1 < last:
                @pl.when(z > 0)
                def _():
                    down(s + 1).start()
            hand(w + 2 * s + 2, nz + s).start()

    def hand_step(s):
        @pl.when(z - 1 - s >= 0)
        def _():
            hand(twin - 2 * s - 2, 1 + s).wait_recv()

        @pl.when(z + 1 + s <= last)
        def _():
            hand(twin + 2 * s + 2, nz + s).wait_recv()

    square = nb == 4
    half = nq * cells // 2
    bx, by = b % 2, b // 2 % 2
    on_x, on_y, across = b + 1 - 2 * bx, b + 2 - 4 * by, nb - 1 - b

    def piece(owner, h, n, where):
        return remote(qall.at[owner, h * half:(h + 1) * half], qs, qr, n, (w, where))

    small = [remote(call_ref.at[b], cs, cr, d, (w, lax.rem(b + d, nb))) for d in range(1, nb)]
    if square:
        first = [piece(b, 0, 0, on_x), piece(b, 1, 2, on_y), piece(b, 1, 1, on_x), piece(b, 0, 3, on_y)]
        onward = [piece(on_x, 0, 4, on_y), piece(on_y, 1, 5, on_x)]
        arrive = [piece(on_x, 0, 0, on_x), piece(on_y, 1, 2, on_y), piece(on_x, 1, 1, on_x),
                  piece(on_y, 0, 3, on_y), piece(across, 0, 4, on_y), piece(across, 1, 5, on_x)]
    else:
        first = [remote(qall.at[b], qs, qr, d, (w, lax.rem(b + d, nb))) for d in range(1, nb)]
        onward = []
        arrive = [remote(qall.at[lax.rem(b + nb - d, nb)], qs, qr, d, (w, lax.rem(b + d, nb)))
                  for d in range(1, nb)]

    @pl.when(z < last)
    def _():
        up(0).start()

    @pl.when(z > 0)
    def _():
        down(0).start()

    loads[1].wait()
    qall[b] = normalize(qin[...]).reshape(nq * cells, depth)
    for c in first:
        c.start()
    hand(w, 0).start()
    for c in loads[2:]:
        c.wait()
    for c in small:
        c.start()

    lane = lax.broadcasted_iota(jnp.int32, (cells, 2 * cells), 1)
    left = lane < cells
    columns = qtab_ref.shape[1]
    taps = qt_in[...].astype(jnp.float32)
    bias = bias_in[...]
    masks = [m & left for m in tap_masks(cells, 2 * cells, True)]
    for k in range(hid):
        b0 = jnp.broadcast_to(bias[:, k:k + 1], (cells, 2 * cells))
        b1 = b0.astype(jnp.bfloat16).astype(jnp.float32)
        b2 = (b0 - b1).astype(jnp.bfloat16).astype(jnp.float32)
        b3 = b0 - b1 - b2
        table = jnp.where(lane == cells, b1, jnp.where(lane == cells + 1, b2, jnp.where(lane == cells + 2, b3, 0.0)))
        for t in range(9):
            table = jnp.where(masks[t], taps[k:k + 1, t:t + 1], table)
        qtab_ref[k * cells:(k + 1) * cells, :] = table.astype(jnp.bfloat16)[:, :columns]
    line_step(0)
    if square:
        for n in range(2):
            arrive[n].wait_recv()
            onward[n].start()
    if last > 1:
        line_step(1)
    taps = rt_in[...].astype(jnp.float32)
    masks = tap_masks(cells, 2 * cells, False)
    rtab_ref[...] = jnp.zeros_like(rtab_ref)
    for k in range(hid):
        table = jnp.zeros((cells, 2 * cells), jnp.float32)
        for t in range(9):
            table = jnp.where(masks[t], taps[k:k + 1, t:t + 1], table)
        for s in range(4):
            row = (k * 4 + s) * cells
            at = s // 2 * 2 * cells
            part = jnp.where(left if s % 2 == 0 else ~left, table, 0.0)
            rtab_ref[row:row + cells, at:at + 2 * cells] = part.astype(jnp.bfloat16)

    tables = [pltpu.make_async_copy(qtab_ref, qtab_hbm, store.at[nb * nz]),
              pltpu.make_async_copy(rtab_ref, rtab_hbm, store.at[nb * nz + 1])]
    for c in tables:
        c.start()
    scale = 1.0 / math.sqrt(depth)
    ones = jnp.ones((columns - cells, nq * nr * cells), jnp.bfloat16)

    def leave(t, far):
        at = pl.ds(t * nw + 2 * far, 2)
        return pltpu.make_async_copy(corr_ref.at[at], corr_hbm.at[at], store.at[t * nz + far])

    def correlate(t, far):
        pair = rall[pl.ds(2 * far, 2)].reshape(2 * nr * cells, depth)
        block = lax.dot_general(qall[t], pair, (((1,), (1,)), ((), ())),
                                preferred_element_type=jnp.float32)
        block = (block * scale).astype(jnp.bfloat16)
        for side in range(2):
            n = t * nw + 2 * far + side
            lanes = slice(side * nr * cells, (side + 1) * nr * cells)
            for p in range(nq):
                corr_ref[n, :cells, p * nr * cells:(p + 1) * nr * cells] = block[p * cells:(p + 1) * cells, lanes]
            corr_ref[n, cells:, :] = ones
        leave(t, far).start()

    early = 3 if square else nb

    def at_distance(d):
        def one(m, carry):
            t, side = m // 2, m % 2
            if square:
                t = (by + t // 2) % 2 * 2 + (bx + t % 2) % 2
            far = z + (side * 2 - 1) * d

            @pl.when((far >= 0) & (far <= last))
            def _():
                correlate(t, far)
            return carry

        def here(m, carry):
            if square:
                m = (by + m // 2) % 2 * 2 + (bx + m % 2) % 2
            correlate(m, z)
            return carry

        if d == 0:
            lax.fori_loop(0, early, here, 0)
        else:
            lax.fori_loop(0, early * 2, one, 0)

    if square:
        arrive[2].wait_recv()
        arrive[3].wait_recv()
    else:
        for c in arrive:
            c.wait_recv()
    hand(twin, 0).wait_recv()
    at_distance(0)
    for d in range(1, nz):
        if d > 2:
            line_step(d - 1)
        hand_step(d - 1)
        at_distance(d)
    if square:
        arrive[4].wait_recv()
        arrive[5].wait_recv()

        def rest(far, carry):
            correlate(across, far)
            return carry
        lax.fori_loop(0, nz, rest, 0)

    for c in small + tables:
        c.wait()
    for c in first + onward:
        c.wait_send()
    hand(w, 0).wait_send()
    for s in range(last):
        @pl.when((z - s >= 0) & (z < last))
        def _():
            up(s).wait_send()

        @pl.when((z + s <= last) & (z > 0))
        def _():
            down(s).wait_send()

        @pl.when(z - 1 - s >= 0)
        def _():
            hand(w - 2 * s - 2, 1 + s).wait_send()

        @pl.when(z + 1 + s <= last)
        def _():
            hand(w + 2 * s + 2, nz + s).wait_send()

    def left_for(n, carry):
        leave(n // nz, n % nz).wait()
        return carry
    lax.fori_loop(0, nb * nz, left_for, 0)


def score_kernel(nw, nb, nq, nr, cells, hid, cand_ref, corr_hbm, qtab_hbm, rtab_hbm, out_ref,
                 corr_ref, qtab_ref, rtab_ref, load, hidden, filtered, items):
    b = lax.axis_index("blk")
    wide = 4 * cells
    loads = [pltpu.make_async_copy(src, dst, load.at[n]) for n, (src, dst) in enumerate((
        (qtab_hbm, qtab_ref), (corr_hbm, corr_ref), (rtab_hbm, rtab_ref)))]
    for c in loads:
        c.start()
    out_ref[...] = jnp.zeros_like(out_ref)

    def scan(n, count):
        flag = cand_ref[n // nw, 0, n % nw] != 0

        @pl.when(flag)
        def _():
            items[count] = n
        return count + jnp.where(flag, 1, 0)

    count = lax.fori_loop(0, nb * nw, scan, jnp.int32(0))
    columns = out_ref.shape[2]
    halves = nq * nr // 4
    row_id = lax.broadcasted_iota(jnp.int32, (nq, columns), 0)
    lane_id = lax.broadcasted_iota(jnp.int32, (nq, columns), 1)
    left = lax.broadcasted_iota(jnp.int32, (cells, 2 * cells), 1) < cells
    left_row = lax.broadcasted_iota(jnp.int32, (1, 2 * cells), 1) < cells

    def pool(item, g):
        t, v = item // nw, item % nw
        base = v * (nb * nr) + b * nr
        result = out_ref[t]
        for p in range(nq):
            row = pl.multiple_of((g * halves + p // 2) * cells, cells)
            lane = p % 2 * 2 * cells
            f = filtered[pl.ds(row, cells), lane:lane + 2 * cells]
            col = jnp.max(f, axis=0, keepdims=True)
            for r in range(2):
                own_f = jnp.where(left if r == 0 else ~left, f, -jnp.inf)
                own_c = jnp.where(left_row if r == 0 else ~left_row, col, 0.0)
                total = (jnp.sum(jnp.max(own_f, axis=1, keepdims=True), axis=0, keepdims=True)
                         + jnp.sum(own_c, axis=1, keepdims=True))
                total = total * (0.5 / cells)
                result = jnp.where((row_id == p) & (lane_id == base + r), total, result)
        out_ref[t] = result

    filtered[...] = jnp.zeros_like(filtered)

    def group(i, carry):
        start = i * GROUP
        size = jnp.minimum(count - start, GROUP)
        past = jnp.maximum(start - GROUP, 0)

        def item(g, inner):
            own = items[start + g]
            for h in range(halves):
                value = jnp.dot(qtab_ref[...], corr_ref[own, :, h * wide:(h + 1) * wide],
                                preferred_element_type=jnp.float32).astype(jnp.bfloat16)
                row = pl.multiple_of((g * halves + h) * cells, cells)
                for k in range(hid):
                    part = value[k * cells:(k + 1) * cells]
                    hidden[pl.ds(row, cells), k * wide:(k + 1) * wide] = jnp.maximum(part, jnp.bfloat16(0.0))
            pool(items[past + g], g)
            return inner

        def only_pool(g, inner):
            pool(items[past + g], g)
            return inner

        lax.fori_loop(0, size, item, 0)
        lax.fori_loop(size, jnp.where(i > 0, GROUP, 0), only_pool, 0)
        filtered[...] = jnp.dot(hidden[...], rtab_ref[...], preferred_element_type=jnp.float32)
        return carry

    for c in loads:
        c.wait()
    groups = (count + GROUP - 1) // GROUP
    lax.fori_loop(0, groups, group, 0)
    final = jnp.maximum(groups - 1, 0) * GROUP

    def last_pool(g, inner):
        pool(items[final + g], g)
        return inner
    lax.fori_loop(0, count - final, last_pool, 0)


def exchange_kernel(nw, nb, s_ref, out_ref, got, ss, sr):
    w, b = lax.axis_index("wide"), lax.axis_index("blk")
    barrier = pltpu.get_barrier_semaphore()
    for d in range(1, nb):
        pl.semaphore_signal(barrier, inc=1, device_id=(w, lax.rem(b + d, nb)), device_id_type=MESH)
    pl.semaphore_wait(barrier, nb - 1)
    copies = []
    for d in range(1, nb):
        to = lax.rem(b + d, nb)
        copies.append(pltpu.make_async_remote_copy(
            src_ref=s_ref.at[to], dst_ref=got.at[d], send_sem=ss.at[d], recv_sem=sr.at[d],
            device_id=(w, to), device_id_type=MESH))
    for c in copies:
        c.start()
    total = s_ref[b]
    for c in copies:
        c.wait()
    for d in range(1, nb):
        total = total + got[d]
    out_ref[...] = total


def shards(nw, nb, queries, references, query_taps, ref_taps, tap_bias, candidates):
    nq, cells, depth = queries.shape
    nr = references.shape[0]
    hid = query_taps.shape[0]
    dma = pltpu.SemaphoreType.DMA
    bf16 = jnp.bfloat16
    depth_in = cells + 16
    nz = nw // 2
    corr, qtab, rtab, cand = pl.pallas_call(
        functools.partial(gather_kernel, nw, nb),
        out_shape=(
            jax.ShapeDtypeStruct((nb * nw, depth_in, nq * nr * cells), bf16),
            jax.ShapeDtypeStruct((hid * cells, depth_in), bf16),
            jax.ShapeDtypeStruct((hid * 4 * cells, 4 * cells), bf16),
            jax.ShapeDtypeStruct((nb, 1, nw), jnp.int32),
        ),
        in_specs=[HBM] * 6,
        out_specs=(HBM, HBM, HBM, VMEM),
        scratch_shapes=[
            pltpu.VMEM((nb * nw, depth_in, nq * nr * cells), bf16),
            pltpu.VMEM((hid * cells, depth_in), bf16),
            pltpu.VMEM((hid * 4 * cells, 4 * cells), bf16),
            dma((nb * nz + 2,)),
            pltpu.VMEM((nb, nq * cells, depth), bf16),
            pltpu.VMEM((nw, nr * cells, depth), bf16),
            pltpu.VMEM(queries.shape, bf16),
            pltpu.VMEM(references.shape, bf16),
            pltpu.VMEM(query_taps.shape, bf16),
            pltpu.VMEM(ref_taps.shape, bf16),
            pltpu.VMEM((1, hid), jnp.float32),
            dma((6,)), dma((max(nb, 6),)), dma((max(nb, 6),)), dma((2 * nz,)), dma((2 * nz,)),
            dma((2 * nz,)), dma((2 * nz,)), dma((nb,)), dma((nb,)),
        ],
        compiler_params=pltpu.CompilerParams(
            collective_id=0, has_side_effects=True, vmem_limit_bytes=56 * 2**20),
        name="gather",
    )(queries, references, query_taps, ref_taps, tap_bias.reshape(1, hid), candidates)
    rows = GROUP * nq * nr // 4 * cells
    scores = pl.pallas_call(
        functools.partial(score_kernel, nw, nb, nq, nr, cells, hid),
        out_shape=jax.ShapeDtypeStruct((nb, nq, nw * nb * nr), jnp.float32),
        in_specs=[SMEM, HBM, HBM, HBM],
        out_specs=VMEM,
        scratch_shapes=[
            pltpu.VMEM(corr.shape, bf16),
            pltpu.VMEM(qtab.shape, bf16),
            pltpu.VMEM(rtab.shape, bf16),
            dma((3,)),
            pltpu.VMEM((rows, hid * 4 * cells), bf16),
            pltpu.VMEM((rows, 4 * cells), jnp.float32),
            pltpu.SMEM((nb * nw,), jnp.int32),
        ],
        compiler_params=pltpu.CompilerParams(vmem_limit_bytes=56 * 2**20),
        name="score",
    )(cand, corr, qtab, rtab)
    return pl.pallas_call(
        functools.partial(exchange_kernel, nw, nb),
        out_shape=jax.ShapeDtypeStruct(scores.shape[1:], jnp.float32),
        in_specs=[VMEM],
        out_specs=VMEM,
        scratch_shapes=[pltpu.VMEM(scores.shape, jnp.float32), dma((nb,)), dma((nb,))],
        compiler_params=pltpu.CompilerParams(
            collective_id=1, has_side_effects=True, vmem_limit_bytes=16 * 2**20),
        name="exchange",
    )(scores)


def solution(mesh):
    nw, nb = mesh.shape["wide"], mesh.shape["blk"]
    placed = (
        P(("wide", "blk"), None, None),
        P(("wide", "blk"), None, None),
        P(),
        P(),
        P(),
        P(("wide", "blk"), None),
    )
    return jax.shard_map(
        functools.partial(shards, nw, nb), mesh=mesh, in_specs=placed,
        out_specs=P(("wide", "blk"), None), check_vma=False,
    )
```
